512 devices in a mesh: fsdp: 64 (over y_hi, z, core), rep: 8 (over x, y_lo).
Axes of the slice: x: 4, y: 4 (y_hi: 2, y_lo: 2; y = y_hi * 2 + y_lo), z: 16, core: 2. Of those that a mesh axis runs over, the one named last changes fastest.
Arguments:
- activations: bfloat16 [131072, 4096], P(('fsdp', 'rep')), may hold values from -6 to 6
- blocks: bfloat16 [64, 128, 128], P('fsdp'), may hold values from -0.1875 to 0.1875
- block_row: int32 [64], P('fsdp'), may hold values from 0 to 31, as said below
- block_column: int32 [64], P('fsdp'), may hold values from 0 to 7, as said below
- cotangent: bfloat16 [131072, 1024], P(('fsdp', 'rep')), may hold values from -6 to 6
Outputs:
- values_out: bfloat16 [131072, 1024], P(('fsdp', 'rep'))
- input_grad: bfloat16 [131072, 4096], P(('fsdp', 'rep'))
- weight_grad: float32 [64, 128, 128], P('fsdp')
The draws below stay inside these ranges and needn't reach their ends.
Inputs may be any that keep to these rules, and one draw needn't show every extreme that they name: `block_row`: every block row holds exactly 2 nonzero blocks and every block column exactly 8; no pair of block row and block column appears twice. `block_column`: taken together with block_row as above.
All inputs are finite; a program needn't handle non-finite values.
Results may differ from the reference program's by a relative error of at most 0.001.
Values may be sent and summed in bfloat16 or wider, within the bound.
No kernel may reach another device: no remote copies, remote signals or barrier semaphores. Data moves between devices by JAX's collectives and lax.ppermute only.
A program may use at most 64 MiB of HBM per device.

```python
import jax
import jax.numpy as jnp
from jax import lax

DIN = 4096
KVW = 1024
BLK = 128
RB = 32
CB = 8
NNZ = 64
TOKENS = 131072


def pattern(key):
    base = jax.random.fold_in(key, 11)
    row_key, col_key, order_key = jax.random.split(base, 3)
    row_labels = jax.random.permutation(row_key, RB)
    col_labels = jax.random.permutation(col_key, CB)
    present = ((row_labels[:, None] + col_labels[None, :]) % 4 == 0).reshape(-1)
    places = jnp.arange(RB * CB, dtype=jnp.int32)
    ranking = jnp.where(present, 0, 1).astype(jnp.int32) * (RB * CB) + places
    chosen = jnp.argsort(ranking, stable=True)[:NNZ].astype(jnp.int32)
    chosen = chosen[jax.random.permutation(order_key, NNZ)]
    return ((chosen // CB).astype(jnp.int32), (chosen % CB).astype(jnp.int32))


def draw_block_row(key, part):
    return pattern(key)[0]


def draw_block_column(key, part):
    return pattern(key)[1]


def block_levels(rng, shape, cuts, least, top_value):
    gain, own = 1.0, jax.random.fold_in(rng, 6)
    for axis_at, shards_of in cuts:
        steps = jnp.exp(jax.random.uniform(jax.random.fold_in(own, axis_at), (shards_of,), jnp.float32, least / len(cuts), top_value / len(cuts)))
        gain = gain * jnp.repeat(steps, shape[axis_at] // shards_of).reshape([-1 if axis == axis_at else 1 for axis in range(len(shape))])
    return gain


def gaussian(rng, shape, scale, most, shards=(), kind=jnp.bfloat16):
    drawn = scale * jax.random.normal(rng, shape, jnp.float32)
    if shards:
        drawn = drawn * block_levels(rng, shape, shards, -0.22, 0.18)
    return jnp.clip(drawn, -most, most).astype(kind)


def setup_inputs(seed: int = 0) -> dict:
    key_of = jax.random.split(jax.random.key(seed), 6)
    activations = gaussian(key_of[0], (TOKENS, DIN), 1.0, 6.0, ((0, 512),))
    blocks = gaussian(key_of[1], (NNZ, BLK, BLK), (DIN // 4) ** -0.5, 0.1875, ((0, 64),))
    block_row = draw_block_row(jax.random.fold_in(key_of[5], 71), 0)
    block_column = draw_block_column(jax.random.fold_in(key_of[5], 71), 0)
    cotangent = gaussian(key_of[4], (TOKENS, KVW), 1.0, 6.0, ((0, 512),))
    return dict(activations=activations, blocks=blocks, block_row=block_row, block_column=block_column, cotangent=cotangent)


def reference(activations, blocks, block_row, block_column, cotangent):
    def one_block(running, index):
        values_acc, grads_acc = running
        row_start = (block_row[index] * BLK).astype(jnp.int32)
        col_start = (block_column[index] * BLK).astype(jnp.int32)
        inputs = lax.dynamic_slice_in_dim(activations, row_start, BLK, 1)
        outgrad = lax.dynamic_slice_in_dim(cotangent, col_start, BLK, 1)
        weight = blocks[index]
        forward = jnp.dot(inputs, weight, preferred_element_type=jnp.float32)
        previous = lax.dynamic_slice_in_dim(values_acc, col_start, BLK, 1)
        values_acc = lax.dynamic_update_slice_in_dim(values_acc, previous + forward, col_start, 1)
        backward = jnp.dot(outgrad, weight.T, preferred_element_type=jnp.float32)
        earlier = lax.dynamic_slice_in_dim(grads_acc, row_start, BLK, 1)
        grads_acc = lax.dynamic_update_slice_in_dim(grads_acc, earlier + backward, row_start, 1)
        block_grad = jnp.dot(inputs.T, outgrad, preferred_element_type=jnp.float32)
        return (values_acc, grads_acc), block_grad

    initial = (jnp.zeros((TOKENS, KVW), jnp.float32), jnp.zeros((TOKENS, DIN), jnp.float32))
    final, block_grads = lax.scan(one_block, initial, jnp.arange(NNZ, dtype=jnp.int32))
    values_out = final[0].astype(jnp.bfloat16)
    input_grad = final[1].astype(jnp.bfloat16)
    weight_grad = block_grads * (TOKENS ** -0.5)
    return values_out, input_grad, weight_grad
```

```python
import functools

import jax
import jax.numpy as jnp
from jax import lax
from jax.experimental import pallas as pl
from jax.experimental.pallas import tpu as pltpu
from jax.sharding import Mesh, PartitionSpec as P

AXES = ("yh", "z", "c", "x", "yl")
SIZES = (2, 16, 2, 4, 2)
FSDP = ("yh", "z", "c")
REP = ("x", "yl")
PLANE = ("yh", "x", "yl")
B = 128
NNZ, RB, CB = 64, 32, 8
VMEM = pltpu.CompilerParams(vmem_limit_bytes=48 * 1024 * 1024)


def grads_kernel(parity_ref, code_ref, x_ref, g_ref, out_ref):
    parity = parity_ref[0]
    for yh in range(2):
        for z in range(16):
            code = code_ref[yh * 32 + z * 2 + parity]
            row = pl.multiple_of((code // CB) * B, B)
            col = pl.multiple_of((code % CB) * B, B)
            grad = lax.dot_general(
                x_ref[:, pl.ds(row, B)],
                g_ref[:, pl.ds(col, B)],
                (((0,), (0,)), ((), ())),
                preferred_element_type=jnp.float32,
            )
            out_ref[yh * 8 : (yh + 1) * 8, z] = grad.reshape(8, 16, B)


def half_grads(parity, codes, x, g):
    smem = pl.BlockSpec(memory_space=pltpu.SMEM)
    vmem = pl.BlockSpec(memory_space=pltpu.VMEM)
    return pl.pallas_call(
        grads_kernel,
        out_shape=jax.ShapeDtypeStruct((16, 16, 16, B), jnp.float32),
        in_specs=[smem, smem, vmem, vmem],
        out_specs=vmem,
        compiler_params=VMEM,
        name="block_grads",
    )(parity.reshape(1), codes, x, g)


def project_kernel(code_ref, x_ref, g_ref, w_ref, v_ref, d_ref, by_col, by_row, fill):
    for k in range(CB):
        fill[k] = 0
    for k in range(RB):
        fill[CB + k] = 0

    def place(n, carry):
        code = code_ref[n]
        row, col = code // CB, code % CB
        at = fill[col]
        by_col[col * 8 + at] = n
        fill[col] = at + 1
        at = fill[CB + row]
        by_row[row * 2 + at] = n
        fill[CB + row] = at + 1
        return carry

    lax.fori_loop(0, NNZ, place, 0)

    def block(n):
        return jnp.concatenate(
            [w_ref[:, pl.ds(pl.multiple_of(n * 512 + i * B, B), B)] for i in range(4)], axis=0
        )

    for col in range(CB):
        ns = [by_col[col * 8 + k] for k in range(8)]
        rows = [code_ref[n] // CB for n in ns]
        xs = jnp.concatenate(
            [x_ref[:, pl.ds(pl.multiple_of(r * B, B), B)] for r in rows], axis=1
        )
        ws = jnp.concatenate([block(n) for n in ns], axis=0)
        v_ref[:, col * B : (col + 1) * B] = jnp.dot(
            xs, ws, preferred_element_type=jnp.float32
        ).astype(v_ref.dtype)
    for row in range(RB):
        ns = [by_row[row * 2 + k] for k in range(2)]
        cols = [code_ref[n] % CB for n in ns]
        gs = jnp.concatenate(
            [g_ref[:, pl.ds(pl.multiple_of(c * B, B), B)] for c in cols], axis=1
        )
        ws = jnp.concatenate([block(n) for n in ns], axis=1)
        d_ref[:, row * B : (row + 1) * B] = lax.dot_general(
            gs, ws, (((1,), (1,)), ((), ())), preferred_element_type=jnp.float32
        ).astype(d_ref.dtype)


def project(codes, x, g, w):
    smem = pl.BlockSpec(memory_space=pltpu.SMEM)
    vmem = pl.BlockSpec(memory_space=pltpu.VMEM)
    return pl.pallas_call(
        project_kernel,
        out_shape=[
            jax.ShapeDtypeStruct(g.shape, jnp.bfloat16),
            jax.ShapeDtypeStruct(x.shape, jnp.bfloat16),
        ],
        in_specs=[smem, vmem, vmem, vmem],
        out_specs=[vmem, vmem],
        scratch_shapes=[
            pltpu.SMEM((NNZ,), jnp.int32),
            pltpu.SMEM((NNZ,), jnp.int32),
            pltpu.SMEM((CB + RB,), jnp.int32),
        ],
        compiler_params=VMEM,
        name="project",
    )(codes, x, g, w)


def to_all(part, axes, count):
    return lax.all_to_all(
        jnp.broadcast_to(part[None], (count,) + part.shape), axes, 0, 0, tiled=True
    )


def per_device(x, blocks, block_row, block_column, g):
    core = lax.axis_index("c")
    rep = lax.axis_index(REP)
    pieces = blocks.reshape(4, 2, 2, 8, B)
    mine = lax.dynamic_index_in_dim(pieces, rep, 3, keepdims=False)
    mine = mine.transpose(2, 1, 0, 3)
    code = (block_row * CB + block_column).astype(jnp.bfloat16)
    tail = jnp.broadcast_to(code.reshape(1, 1, 1, 1), (2, 2, 4, B))
    packet = jnp.concatenate([mine, tail], axis=2)
    packet = jnp.broadcast_to(packet[:, None], (2, 16, 2, 8, B)).reshape(64, 8, B)
    got = lax.all_to_all(packet, FSDP, 0, 0, tiled=True)
    codes = got[:, 4, 0].astype(jnp.int32)
    share = got[:, :4, :].reshape(NNZ * 512)

    other = half_grads(1 - core, codes, x, g)
    swap = [(0, 1), (1, 0)]
    incoming = lax.ppermute(other, "c", swap)
    own = half_grads(core, codes, x, g)
    paired = own + incoming
    spread = lax.all_to_all(paired, PLANE, 0, 0, tiled=True)
    plane_sum = jnp.sum(spread, axis=0)

    half_w = to_all(share, PLANE, 16)
    far_w = lax.ppermute(half_w, "c", swap)
    low = jnp.where(core == 0, half_w, far_w)
    high = jnp.where(core == 0, far_w, half_w)
    w = jnp.concatenate([low, high], axis=0)
    values_out, input_grad = project(codes, x, g, w)

    ring = lax.all_to_all(plane_sum, "z", 0, 0, tiled=True)
    strip = jnp.sum(ring, axis=0)
    whole = to_all(strip, REP, 8)
    loss_scale = (x.shape[0] * lax.axis_size(AXES)) ** (-0.5)
    weight_grad = whole.reshape(1, B, B) * loss_scale
    return values_out, input_grad, weight_grad


def solution(mesh):
    cut = Mesh(mesh.devices.reshape(SIZES), AXES)
    in_specs = (P(AXES, None), P(FSDP, None, None), P(FSDP), P(FSDP), P(AXES, None))
    out_specs = (P(AXES, None), P(AXES, None), P(FSDP, None, None))
    return jax.shard_map(
        per_device, mesh=cut, in_specs=in_specs, out_specs=out_specs, check_vma=False
    )
```

```python
import functools

import jax
import jax.numpy as jnp
from jax import lax
from jax.experimental import pallas as pl
from jax.experimental.pallas import tpu as pltpu
from jax.sharding import Mesh, PartitionSpec as P

AXES = ("yh", "z", "c", "x", "yl")
SIZES = (2, 16, 2, 4, 2)
FSDP = ("yh", "z", "c")
REP = ("x", "yl")
PLANE = ("yh", "x", "yl")
B = 128
NNZ, RB, CB = 64, 32, 8


def vmem_mib(limit):
    return pltpu.CompilerParams(vmem_limit_bytes=limit * 1024 * 1024)


def grads_kernel(parity_ref, code_ref, x_ref, g_ref, out_ref):
    parity = parity_ref[0]
    for yh in range(2):
        for z in range(16):
            code = code_ref[yh * 32 + z * 2 + parity]
            row = pl.multiple_of((code // CB) * B, B)
            col = pl.multiple_of((code % CB) * B, B)
            grad = lax.dot_general(
                x_ref[:, pl.ds(row, B)],
                g_ref[:, pl.ds(col, B)],
                (((0,), (0,)), ((), ())),
                preferred_element_type=jnp.float32,
            )
            out_ref[yh * 8 : (yh + 1) * 8, z] = grad.reshape(8, 16, B)


def half_grads(parity, codes, x, g):
    smem = pl.BlockSpec(memory_space=pltpu.SMEM)
    vmem = pl.BlockSpec(memory_space=pltpu.VMEM)
    return pl.pallas_call(
        grads_kernel,
        out_shape=jax.ShapeDtypeStruct((16, 16, 16, B), jnp.float32),
        in_specs=[smem, smem, vmem, vmem],
        out_specs=vmem,
        compiler_params=vmem_mib(8),
        name="block_grads",
    )(parity.reshape(1), codes, x, g)


def share_kernel(got_ref, power_ref, share_ref, wide):
    wide[...] = got_ref[...].astype(jnp.float32).reshape(NNZ * 4, B)
    power = jnp.concatenate([power_ref[...]] * 2, axis=0).astype(jnp.bfloat16)
    for i in range(2):
        rows = wide[pl.ds(i, NNZ, stride=4), :].astype(jnp.bfloat16)
        for copy in range(16):
            share_ref[copy, i * NNZ : (i + 1) * NNZ, :] = rows
    for copy in range(16):
        share_ref[copy, 2 * NNZ :, :] = power


def share_copies(got, power):
    vmem = pl.BlockSpec(memory_space=pltpu.VMEM)
    return pl.pallas_call(
        share_kernel,
        out_shape=jax.ShapeDtypeStruct((16, 2 * NNZ + 16, B), jnp.bfloat16),
        in_specs=[vmem, vmem],
        out_specs=vmem,
        scratch_shapes=[pltpu.VMEM((NNZ * 4, B), jnp.float32)],
        compiler_params=vmem_mib(4),
        name="share",
    )(got, power)


def project_kernel(place_ref, code_ref, x_ref, g_ref, w00_ref, w01_ref, w1_ref, v_ref, d_ref, by_col, by_row, fill, wide, w):
    core, odd = place_ref[0], place_ref[1]
    for s in range(16):
        for c_ref, at in (
            (w00_ref.at[s], core * 32 + odd * 16 + s),
            (w01_ref.at[s], core * 32 + (1 - odd) * 16 + s),
            (w1_ref.at[0, s], (1 - core) * 32 + odd * 16 + s),
            (w1_ref.at[1, s], (1 - core) * 32 + (1 - odd) * 16 + s),
        ):
            wide[pl.ds(pl.multiple_of(at * 128, 128), 128), :] = c_ref[: 2 * NNZ].astype(
                jnp.float32
            )
    for n in range(NNZ):
        for i in range(2):
            w[n, i * 64 : (i + 1) * 64, :] = wide[
                pl.ds(i * NNZ + n, 64, stride=128), :
            ].astype(jnp.bfloat16)

    for k in range(CB + RB):
        fill[k] = 0

    def place(n, carry):
        code = code_ref[n]
        row, col = code // CB, code % CB
        at = fill[col]
        by_col[col * 8 + at] = n
        fill[col] = at + 1
        at = fill[CB + row]
        by_row[row * 2 + at] = n
        fill[CB + row] = at + 1
        return carry

    lax.fori_loop(0, NNZ, place, 0)

    for col in range(CB):
        ns = [by_col[col * 8 + k] for k in range(8)]
        rows = [code_ref[n] // CB for n in ns]
        xs = jnp.concatenate(
            [x_ref[:, pl.ds(pl.multiple_of(r * B, B), B)] for r in rows], axis=1
        )
        ws = jnp.concatenate([w[n] for n in ns], axis=0)
        v_ref[:, col * B : (col + 1) * B] = jnp.dot(
            xs, ws, preferred_element_type=jnp.float32
        ).astype(v_ref.dtype)
    for row in range(RB):
        ns = [by_row[row * 2 + k] for k in range(2)]
        cols = [code_ref[n] % CB for n in ns]
        gs = jnp.concatenate(
            [g_ref[:, pl.ds(pl.multiple_of(c * B, B), B)] for c in cols], axis=1
        )
        ws = jnp.concatenate([w[n] for n in ns], axis=1)
        d_ref[:, row * B : (row + 1) * B] = lax.dot_general(
            gs, ws, (((1,), (1,)), ((), ())), preferred_element_type=jnp.float32
        ).astype(d_ref.dtype)


def project(place, codes, x, g, near, next_to, far):
    smem = pl.BlockSpec(memory_space=pltpu.SMEM)
    vmem = pl.BlockSpec(memory_space=pltpu.VMEM)
    return pl.pallas_call(
        project_kernel,
        out_shape=[
            jax.ShapeDtypeStruct(g.shape, jnp.bfloat16),
            jax.ShapeDtypeStruct(x.shape, jnp.bfloat16),
        ],
        in_specs=[smem, smem, vmem, vmem, vmem, vmem, vmem],
        out_specs=[vmem, vmem],
        scratch_shapes=[
            pltpu.SMEM((NNZ,), jnp.int32),
            pltpu.SMEM((NNZ,), jnp.int32),
            pltpu.SMEM((CB + RB,), jnp.int32),
            pltpu.VMEM((32 * 256, B), jnp.float32),
            pltpu.VMEM((NNZ, B, B), jnp.bfloat16),
        ],
        compiler_params=vmem_mib(20),
        name="project",
    )(place, codes, x, g, near, next_to, far)


def flip(value, axis, by=1):
    size = lax.axis_size(axis)
    return lax.ppermute(value, axis, [(i, i ^ by) for i in range(size)])


def to_all(part, axes, count):
    return lax.all_to_all(
        jnp.broadcast_to(part[None], (count,) + part.shape), axes, 0, 0, tiled=True
    )


def per_device(x, blocks, block_row, block_column, g):
    core = lax.axis_index("c")
    rep = lax.axis_index(REP)
    pieces = blocks.reshape(2, 2, 2, 2, 8, B)
    mine = lax.dynamic_index_in_dim(pieces, rep, 4, keepdims=False)
    mine = mine.transpose(3, 2, 1, 0, 4)
    code = (block_row * CB + block_column).astype(jnp.bfloat16)
    tail = jnp.broadcast_to(code.reshape(1, 1, 1, 1, 1), (2, 2, 2, 2, B))
    packet = jnp.concatenate([mine, tail], axis=3)[:, None]
    packet = jnp.broadcast_to(packet, (2, 8, 2, 2, 4, B)).reshape(NNZ, 4, B)
    got = lax.all_to_all(packet, FSDP, 0, 0, tiled=True)
    top = jnp.max(jnp.abs(x)).astype(jnp.float32) * jnp.max(jnp.abs(g)).astype(jnp.float32)
    power = jnp.floor(jnp.log2(16384.0 / (x.shape[0] * jnp.maximum(top, 1e-30))))
    power = jnp.broadcast_to(power, (8, B))
    power = jnp.minimum(power, flip(power, "c"))

    got, power = lax.optimization_barrier((got, power))
    share = share_copies(got, power)
    codes = got[:, 2, 0].astype(jnp.int32)
    share, codes = lax.optimization_barrier((share, codes))
    near = lax.all_to_all(share, PLANE, 0, 0, tiled=True)

    incoming = flip(half_grads(1 - core, codes, x, g), "c")
    own = half_grads(core, codes, x, g)
    paired = ((own + incoming) * jnp.exp2(power[0, 0])).astype(jnp.float16)
    spread = lax.all_to_all(paired, PLANE, 0, 0, tiled=True)
    down = jnp.exp2(-near[:, 2 * NNZ, 0].astype(jnp.float32))
    plane_sum = jnp.sum(spread.astype(jnp.float32) * down[:, None, None, None], axis=0)

    next_to = flip(near, "z")
    far = flip(jnp.stack([near, next_to]), "c")
    place = jnp.stack([core, lax.axis_index("z") % 2]).astype(jnp.int32)
    values_out, input_grad = project(place, codes, x, g, near, next_to, far)

    ring = lax.all_to_all(plane_sum, "z", 0, 0, tiled=True)
    strip = jnp.sum(ring, axis=0)
    strip, values_out = lax.optimization_barrier((strip, values_out))
    whole = to_all(strip, REP, 8)
    loss_scale = (x.shape[0] * lax.axis_size(AXES)) ** (-0.5)
    weight_grad = whole.reshape(1, B, B) * loss_scale
    return values_out, input_grad, weight_grad


def solution(mesh):
    cut = Mesh(mesh.devices.reshape(SIZES), AXES)
    in_specs = (P(AXES, None), P(FSDP, None, None), P(FSDP), P(FSDP), P(AXES, None))
    out_specs = (P(AXES, None), P(AXES, None), P(FSDP, None, None))
    return jax.shard_map(
        per_device, mesh=cut, in_specs=in_specs, out_specs=out_specs, check_vma=False
    )
```

```python
import functools

import jax
import jax.numpy as jnp
from jax import lax
from jax.experimental import pallas as pl
from jax.experimental.pallas import tpu as pltpu
from jax.sharding import Mesh, PartitionSpec as P

AXES = ("yh", "z", "c", "x", "yl")
SIZES = (2, 16, 2, 4, 2)
FSDP = ("yh", "z", "c")
REP = ("x", "yl")
PLANE = ("yh", "x", "yl")
B = 128
NNZ, RB, CB = 64, 32, 8


def vmem_mib(limit):
    return pltpu.CompilerParams(vmem_limit_bytes=limit * 1024 * 1024)


def grads_kernel(parity_ref, code_ref, x_ref, g_ref, out_ref):
    parity = parity_ref[0]
    for yh in range(2):
        for z in range(16):
            code = code_ref[yh * 32 + z * 2 + parity]
            row = pl.multiple_of((code // CB) * B, B)
            col = pl.multiple_of((code % CB) * B, B)
            grad = lax.dot_general(
                x_ref[:, pl.ds(row, B)],
                g_ref[:, pl.ds(col, B)],
                (((0,), (0,)), ((), ())),
                preferred_element_type=jnp.float32,
            )
            out_ref[yh * 8 : (yh + 1) * 8, z] = grad.reshape(8, 16, B)


def half_grads(parity, codes, x, g):
    smem = pl.BlockSpec(memory_space=pltpu.SMEM)
    vmem = pl.BlockSpec(memory_space=pltpu.VMEM)
    return pl.pallas_call(
        grads_kernel,
        out_shape=jax.ShapeDtypeStruct((16, 16, 16, B), jnp.float32),
        in_specs=[smem, smem, vmem, vmem],
        out_specs=vmem,
        compiler_params=vmem_mib(8),
        name="block_grads",
    )(parity.reshape(1), codes, x, g)


def share_kernel(got_ref, power_ref, share_ref, wide):
    wide[...] = got_ref[...].astype(jnp.float32).reshape(NNZ * 4, B)
    power = jnp.concatenate([power_ref[...]] * 2, axis=0).astype(jnp.bfloat16)
    for i in range(2):
        rows = wide[pl.ds(i, NNZ, stride=4), :].astype(jnp.bfloat16)
        for copy in range(16):
            share_ref[copy, i * NNZ : (i + 1) * NNZ, :] = rows
    for copy in range(16):
        share_ref[copy, 2 * NNZ :, :] = power


def share_copies(got, power):
    vmem = pl.BlockSpec(memory_space=pltpu.VMEM)
    return pl.pallas_call(
        share_kernel,
        out_shape=jax.ShapeDtypeStruct((16, 2 * NNZ + 16, B), jnp.bfloat16),
        in_specs=[vmem, vmem],
        out_specs=vmem,
        scratch_shapes=[pltpu.VMEM((NNZ * 4, B), jnp.float32)],
        compiler_params=vmem_mib(4),
        name="share",
    )(got, power)


def stage_kernel(parity_ref, near_ref, next_ref, w_ref, wide):
    for slots, at in ((near_ref, parity_ref[0]), (next_ref, 1 - parity_ref[0])):
        for s in range(16):
            wide[pl.ds(pl.multiple_of((at * 16 + s) * B, B), B), :] = slots[s, :B].astype(
                jnp.float32
            )
    for n in range(NNZ):
        for i in range(2):
            w_ref[n, i * 32 : (i + 1) * 32, :] = wide[
                pl.ds(i * NNZ + n, 32, stride=B), :
            ].astype(jnp.bfloat16)


def stage(parity, near, next_to):
    vmem = pl.BlockSpec(memory_space=pltpu.VMEM)
    return pl.pallas_call(
        stage_kernel,
        out_shape=jax.ShapeDtypeStruct((NNZ, B // 2, B), jnp.bfloat16),
        in_specs=[pl.BlockSpec(memory_space=pltpu.SMEM), vmem, vmem],
        out_specs=vmem,
        scratch_shapes=[pltpu.VMEM((32 * B, B), jnp.float32)],
        compiler_params=vmem_mib(8),
        name="stage",
    )(parity, near, next_to)


def project_kernel(core_ref, code_ref, x_ref, g_ref, near_ref, far_ref, v_ref, d_ref, by_col, by_row, fill, w):
    for half_ref, core in ((near_ref, core_ref[0]), (far_ref, 1 - core_ref[0])):
        for i in range(2):
            at = pl.multiple_of(i * 64 + core * 32, 32)
            w[:, pl.ds(at, 32), :] = half_ref[:, i * 32 : (i + 1) * 32, :]

    for k in range(CB + RB):
        fill[k] = 0

    def place(n, carry):
        code = code_ref[n]
        row, col = code // CB, code % CB
        at = fill[col]
        by_col[col * 8 + at] = n
        fill[col] = at + 1
        at = fill[CB + row]
        by_row[row * 2 + at] = n
        fill[CB + row] = at + 1
        return carry

    lax.fori_loop(0, NNZ, place, 0)

    for col in range(CB):
        ns = [by_col[col * 8 + k] for k in range(8)]
        rows = [code_ref[n] // CB for n in ns]
        xs = jnp.concatenate(
            [x_ref[:, pl.ds(pl.multiple_of(r * B, B), B)] for r in rows], axis=1
        )
        ws = jnp.concatenate([w[n] for n in ns], axis=0)
        v_ref[:, col * B : (col + 1) * B] = jnp.dot(
            xs, ws, preferred_element_type=jnp.float32
        ).astype(v_ref.dtype)
    for row in range(RB):
        ns = [by_row[row * 2 + k] for k in range(2)]
        cols = [code_ref[n] % CB for n in ns]
        gs = jnp.concatenate(
            [g_ref[:, pl.ds(pl.multiple_of(c * B, B), B)] for c in cols], axis=1
        )
        ws = jnp.concatenate([w[n] for n in ns], axis=1)
        d_ref[:, row * B : (row + 1) * B] = lax.dot_general(
            gs, ws, (((1,), (1,)), ((), ())), preferred_element_type=jnp.float32
        ).astype(d_ref.dtype)


def project(place, codes, x, g, near, far):
    smem = pl.BlockSpec(memory_space=pltpu.SMEM)
    vmem = pl.BlockSpec(memory_space=pltpu.VMEM)
    return pl.pallas_call(
        project_kernel,
        out_shape=[
            jax.ShapeDtypeStruct(g.shape, jnp.bfloat16),
            jax.ShapeDtypeStruct(x.shape, jnp.bfloat16),
        ],
        in_specs=[smem, smem, vmem, vmem, vmem, vmem],
        out_specs=[vmem, vmem],
        scratch_shapes=[
            pltpu.SMEM((NNZ,), jnp.int32),
            pltpu.SMEM((NNZ,), jnp.int32),
            pltpu.SMEM((CB + RB,), jnp.int32),
            pltpu.VMEM((NNZ, B, B), jnp.bfloat16),
        ],
        compiler_params=vmem_mib(20),
        cost_estimate=pl.CostEstimate(flops=1, transcendentals=0, bytes_accessed=1),
        name="project",
    )(place, codes, x, g, near, far)


def flip(value, axis, by=1):
    size = lax.axis_size(axis)
    return lax.ppermute(value, axis, [(i, i ^ by) for i in range(size)])


def to_all(part, axes, count):
    return lax.all_to_all(
        jnp.broadcast_to(part[None], (count,) + part.shape), axes, 0, 0, tiled=True
    )


def per_device(x, blocks, block_row, block_column, g):
    core = lax.axis_index("c").astype(jnp.int32)
    rep = lax.axis_index(REP)
    pieces = blocks.reshape(2, 2, 2, 2, 8, B)
    mine = lax.dynamic_index_in_dim(pieces, rep, 4, keepdims=False)
    mine = mine.transpose(3, 2, 1, 0, 4)
    code = (block_row * CB + block_column).astype(jnp.bfloat16)
    tail = jnp.broadcast_to(code.reshape(1, 1, 1, 1, 1), (2, 2, 2, 2, B))
    packet = jnp.concatenate([mine, tail], axis=3)[:, None]
    packet = jnp.broadcast_to(packet, (2, 8, 2, 2, 4, B)).reshape(NNZ, 4, B)
    got = lax.all_to_all(packet, FSDP, 0, 0, tiled=True)

    top = jnp.max(jnp.abs(x)).astype(jnp.float32) * jnp.max(jnp.abs(g)).astype(jnp.float32)
    power = jnp.floor(jnp.log2(16384.0 / (x.shape[0] * jnp.maximum(top, 1e-30))))
    power = jnp.broadcast_to(power, (16, B))
    power = jnp.minimum(power, flip(power, "c"))
    got, power = lax.optimization_barrier((got, power))

    share = share_copies(got, power[:8])
    near = lax.all_to_all(share, PLANE, 0, 0, tiled=True)

    def grads(got, power, x, g):
        codes = got[:, 2, 0].astype(jnp.int32)
        up = jnp.exp2(power)
        outgoing = (half_grads(1 - core, codes, x, g) * up).astype(jnp.float16)
        incoming = flip(outgoing, "c").astype(jnp.float32)
        own = half_grads(core, codes, x, g)
        return (own * up + incoming).astype(jnp.float16), codes

    def nothing(got, power, x, g):
        return jnp.zeros((16, 16, 16, B), jnp.float16), jnp.zeros((NNZ,), jnp.int32)

    paired, codes = lax.cond(block_row[0] < RB, grads, nothing, got, power, x, g)
    paired, near = lax.optimization_barrier((paired, near))
    spread = lax.all_to_all(paired, PLANE, 0, 0, tiled=True)
    down = jnp.exp2(-near[:, B:].astype(jnp.float32))
    plane_sum = jnp.sum(spread.astype(jnp.float32) * down[:, None], axis=0)

    parity = (lax.axis_index("z") % 2).astype(jnp.int32).reshape(1)
    half = stage(parity, near, flip(near, "z"))
    values_out, input_grad = project(core.reshape(1), codes, x, g, half, flip(half, "c"))

    ring = lax.all_to_all(plane_sum, "z", 0, 0, tiled=True)
    ring, values_out = lax.optimization_barrier((ring, values_out))
    strip = jnp.sum(ring, axis=0)
    whole = to_all(strip, REP, 8)
    loss_scale = (x.shape[0] * lax.axis_size(AXES)) ** (-0.5)
    weight_grad = whole.reshape(1, B, B) * loss_scale
    return values_out, input_grad, weight_grad


def solution(mesh):
    cut = Mesh(mesh.devices.reshape(SIZES), AXES)
    in_specs = (P(AXES, None), P(FSDP, None, None), P(FSDP), P(FSDP), P(AXES, None))
    out_specs = (P(AXES, None), P(AXES, None), P(FSDP, None, None))
    return jax.shard_map(
        per_device, mesh=cut, in_specs=in_specs, out_specs=out_specs, check_vma=False
    )
```

```python
import functools

import jax
import jax.numpy as jnp
from jax import lax
from jax.experimental import pallas as pl
from jax.experimental.pallas import tpu as pltpu
from jax.sharding import Mesh, PartitionSpec as P

AXES = ("yh", "z", "c", "x", "yl")
SIZES = (2, 16, 2, 4, 2)
FSDP = ("yh", "z", "c")
REP = ("x", "yl")
PLANE = ("yh", "x", "yl")
B = 128
NNZ, RB, CB = 64, 32, 8


def vmem_mib(limit):
    return pltpu.CompilerParams(vmem_limit_bytes=limit * 1024 * 1024)


def grads_kernel(parity_ref, code_ref, x_ref, g_ref, out_ref):
    parity = parity_ref[0]
    for yh in range(2):
        for z in range(16):
            code = code_ref[yh * 32 + z * 2 + parity]
            row = pl.multiple_of((code // CB) * B, B)
            col = pl.multiple_of((code % CB) * B, B)
            grad = lax.dot_general(
                x_ref[:, pl.ds(row, B)],
                g_ref[:, pl.ds(col, B)],
                (((0,), (0,)), ((), ())),
                preferred_element_type=jnp.float32,
            )
            out_ref[yh * 8 : (yh + 1) * 8, z] = grad.reshape(8, 16, B)


def packet_kernel(rep_ref, row_ref, column_ref, blocks_ref, out_ref, wide):
    wide[...] = blocks_ref[0].astype(jnp.float32)
    code = jnp.full((2, B), row_ref[0] * CB + column_ref[0], jnp.int32).astype(jnp.float32)
    for yh in range(2):
        for odd in range(2):
            for core in range(2):
                at = core * 32 + odd * 16 + yh * 8 + rep_ref[0]
                rows = [wide[pl.ds(at, 1), :], wide[pl.ds(64 + at, 1), :], code]
                piece = jnp.concatenate(rows, axis=0).astype(jnp.bfloat16)
                for z in range(odd, 16, 2):
                    out_ref[yh * 32 + z * 2 + core] = piece


def make_packet(rep, row, column, blocks):
    smem = pl.BlockSpec(memory_space=pltpu.SMEM)
    vmem = pl.BlockSpec(memory_space=pltpu.VMEM)
    return pl.pallas_call(
        packet_kernel,
        out_shape=jax.ShapeDtypeStruct((NNZ, 4, B), jnp.bfloat16),
        in_specs=[smem, smem, smem, vmem],
        out_specs=vmem,
        scratch_shapes=[pltpu.VMEM((B, B), jnp.float32)],
        compiler_params=vmem_mib(4),
        name="packet",
    )(rep, row, column, blocks)


def power_kernel(x_ref, g_ref, out_ref):
    tops = []
    for ref in (x_ref, g_ref):
        top = jnp.abs(ref[:16, :])
        for row in range(16, ref.shape[0], 16):
            top = jnp.maximum(top, jnp.abs(ref[row : row + 16, :]))
        tops.append(jnp.max(top.astype(jnp.float32), axis=(0, 1), keepdims=True))
    bound = x_ref.shape[0] * jnp.maximum(tops[0] * tops[1], 1e-30)
    power = jnp.floor(jnp.log2(16384.0 / bound))
    out_ref[...] = jnp.broadcast_to(power, out_ref.shape)


def own_power(x, g):
    vmem = pl.BlockSpec(memory_space=pltpu.VMEM)
    return pl.pallas_call(
        power_kernel,
        out_shape=jax.ShapeDtypeStruct((16, B), jnp.float32),
        in_specs=[vmem, vmem],
        out_specs=vmem,
        compiler_params=vmem_mib(8),
        name="power",
    )(x, g)


def half_grads(parity, codes, x, g):
    smem = pl.BlockSpec(memory_space=pltpu.SMEM)
    vmem = pl.BlockSpec(memory_space=pltpu.VMEM)
    return pl.pallas_call(
        grads_kernel,
        out_shape=jax.ShapeDtypeStruct((16, 16, 16, B), jnp.float32),
        in_specs=[smem, smem, vmem, vmem],
        out_specs=vmem,
        compiler_params=vmem_mib(8),
        name="block_grads",
    )(parity.reshape(1), codes, x, g)


def share_kernel(got_ref, power_ref, share_ref, wide):
    wide[...] = got_ref[...].astype(jnp.float32).reshape(NNZ * 4, B)
    power = jnp.concatenate([power_ref[...]] * 2, axis=0).astype(jnp.bfloat16)
    for i in range(2):
        rows = wide[pl.ds(i, NNZ, stride=4), :].astype(jnp.bfloat16)
        for copy in range(16):
            share_ref[copy, i * NNZ : (i + 1) * NNZ, :] = rows
    for copy in range(16):
        share_ref[copy, 2 * NNZ :, :] = power


def share_copies(got, power):
    vmem = pl.BlockSpec(memory_space=pltpu.VMEM)
    return pl.pallas_call(
        share_kernel,
        out_shape=jax.ShapeDtypeStruct((16, 2 * NNZ + 16, B), jnp.bfloat16),
        in_specs=[vmem, vmem],
        out_specs=vmem,
        scratch_shapes=[pltpu.VMEM((NNZ * 4, B), jnp.float32)],
        compiler_params=vmem_mib(4),
        name="share",
    )(got, power)


def stage_kernel(parity_ref, near_ref, up_ref, down_ref, w_ref, wide):
    for s in range(16):
        beside = (up_ref if s < 8 else down_ref).at[s % 8]
        for slot, at in ((near_ref.at[s], parity_ref[0]), (beside, 1 - parity_ref[0])):
            wide[pl.ds(pl.multiple_of((at * 16 + s) * B, B), B), :] = slot[:B].astype(
                jnp.float32
            )
    for n in range(NNZ):
        for i in range(2):
            w_ref[n, i * 32 : (i + 1) * 32, :] = wide[
                pl.ds(i * NNZ + n, 32, stride=B), :
            ].astype(jnp.bfloat16)


def stage(parity, near, up, down):
    vmem = pl.BlockSpec(memory_space=pltpu.VMEM)
    smem = pl.BlockSpec(memory_space=pltpu.SMEM)
    return pl.pallas_call(
        stage_kernel,
        out_shape=jax.ShapeDtypeStruct((NNZ, B // 2, B), jnp.bfloat16),
        in_specs=[smem, vmem, vmem, vmem],
        out_specs=vmem,
        scratch_shapes=[pltpu.VMEM((32 * B, B), jnp.float32)],
        compiler_params=vmem_mib(8),
        name="stage",
    )(parity, near, up, down)


def project_kernel(core_ref, code_ref, x_ref, g_ref, near_ref, far_ref, v_out, d_out, by_col, by_row, fill, w, v, d, sems):
    for k in range(CB + RB):
        fill[k] = 0
    for n in range(NNZ):
        code = code_ref[n]
        row, col = code // CB, code % CB
        at = fill[col]
        by_col[col * 8 + at] = n
        fill[col] = at + 1
        at = fill[CB + row]
        by_row[row * 2 + at] = n
        fill[CB + row] = at + 1

    for half_ref, core in ((near_ref, core_ref[0]), (far_ref, 1 - core_ref[0])):
        for i in range(2):
            at = pl.multiple_of(i * 64 + core * 32, 32)
            w[:, pl.ds(at, 32), :] = half_ref[:, i * 32 : (i + 1) * 32, :]

    copies = []
    for row in range(RB):
        ns = [by_row[row * 2 + k] for k in range(2)]
        cols = [code_ref[n] % CB for n in ns]
        gs = jnp.concatenate(
            [g_ref[:, pl.ds(pl.multiple_of(c * B, B), B)] for c in cols], axis=1
        )
        ws = jnp.concatenate([w[n] for n in ns], axis=1)
        d[:, row * B : (row + 1) * B] = lax.dot_general(
            gs, ws, (((1,), (1,)), ((), ())), preferred_element_type=jnp.float32
        ).astype(d.dtype)
        if row % 8 == 7:
            span = pl.ds((row - 7) * B, 8 * B)
            copies.append(
                pltpu.make_async_copy(d.at[:, span], d_out.at[:, span], sems.at[row // 8])
            )
            copies[-1].start()
    for col in range(CB):
        ns = [by_col[col * 8 + k] for k in range(8)]
        rows = [code_ref[n] // CB for n in ns]
        xs = jnp.concatenate(
            [x_ref[:, pl.ds(pl.multiple_of(r * B, B), B)] for r in rows], axis=1
        )
        ws = jnp.concatenate([w[n] for n in ns], axis=0)
        v[:, col * B : (col + 1) * B] = jnp.dot(
            xs, ws, preferred_element_type=jnp.float32
        ).astype(v.dtype)
        if col % 4 == 3:
            span = pl.ds((col - 3) * B, 4 * B)
            copies.append(
                pltpu.make_async_copy(v.at[:, span], v_out.at[:, span], sems.at[4 + col // 4])
            )
            copies[-1].start()
    for copy in copies:
        copy.wait()


def project(core, codes, x, g, near, far):
    smem = pl.BlockSpec(memory_space=pltpu.SMEM)
    vmem = pl.BlockSpec(memory_space=pltpu.VMEM)
    hbm = pl.BlockSpec(memory_space=pl.ANY)
    return pl.pallas_call(
        project_kernel,
        out_shape=[
            jax.ShapeDtypeStruct(g.shape, jnp.bfloat16),
            jax.ShapeDtypeStruct(x.shape, jnp.bfloat16),
        ],
        in_specs=[smem] * 2 + [vmem] * 4,
        out_specs=[hbm, hbm],
        scratch_shapes=[
            pltpu.SMEM((NNZ,), jnp.int32),
            pltpu.SMEM((NNZ,), jnp.int32),
            pltpu.SMEM((CB + RB,), jnp.int32),
            pltpu.VMEM((NNZ, B, B), jnp.bfloat16),
            pltpu.VMEM(g.shape, jnp.bfloat16),
            pltpu.VMEM(x.shape, jnp.bfloat16),
            pltpu.SemaphoreType.DMA((6,)),
        ],
        compiler_params=vmem_mib(20),
        name="project",
    )(core, codes, x, g, near, far)


def flip(value, axis, by=1):
    size = lax.axis_size(axis)
    return lax.ppermute(value, axis, [(i, i ^ by) for i in range(size)])


def to_all(part, axes, count):
    return lax.all_to_all(
        jnp.broadcast_to(part[None], (count,) + part.shape), axes, 0, 0, tiled=True
    )


def per_device(x, blocks, block_row, block_column, g):
    core = lax.axis_index("c").astype(jnp.int32)
    rep = lax.axis_index(REP).astype(jnp.int32).reshape(1)
    packet = make_packet(rep, block_row, block_column, blocks)
    got = lax.all_to_all(packet, FSDP, 0, 0, tiled=True)

    power = own_power(x, g)
    power = jnp.minimum(power, flip(power, "c"))
    got, power = lax.optimization_barrier((got, power))

    share = share_copies(got, power[:8])
    near = lax.all_to_all(share, PLANE, 0, 0, tiled=True)

    def grads(got, power, x, g):
        codes = got[:, 2, 0].astype(jnp.int32)
        up = jnp.exp2(power)
        outgoing = (half_grads(1 - core, codes, x, g) * up).astype(jnp.float16)
        incoming = flip(outgoing, "c").astype(jnp.float32)
        own = half_grads(core, codes, x, g)
        return (own * up + incoming).astype(jnp.float16), codes

    def nothing(got, power, x, g):
        return jnp.zeros((16, 16, 16, B), jnp.float16), jnp.zeros((NNZ,), jnp.int32)

    paired, codes = lax.cond(block_row[0] < RB, grads, nothing, got, power, x, g)
    paired, near = lax.optimization_barrier((paired, near))
    spread = lax.all_to_all(paired, PLANE, 0, 0, tiled=True)
    down = jnp.exp2(-near[:, B:].astype(jnp.float32))
    plane_sum = jnp.sum(spread.astype(jnp.float32) * down[:, None], axis=0)

    parity = (lax.axis_index("z") % 2).astype(jnp.int32).reshape(1)
    from_below = lax.ppermute(near[:8], "z", [(i, (i + 1) % 16) for i in range(16)])
    from_above = lax.ppermute(near[8:], "z", [(i, (i - 1) % 16) for i in range(16)])
    half = stage(parity, near, from_below, from_above)
    far = flip(half, "c")
    values_out, input_grad = project(core.reshape(1), codes, x, g, half, far)

    ring = lax.all_to_all(plane_sum, "z", 0, 0, tiled=True)
    ring, values_out = lax.optimization_barrier((ring, values_out))
    loss_scale = (x.shape[0] * lax.axis_size(AXES)) ** (-0.5)
    strip = jnp.sum(ring, axis=0) * loss_scale
    weight_grad = to_all(strip, REP, 8).reshape(1, B, B)
    return values_out, input_grad, weight_grad


def solution(mesh):
    cut = Mesh(mesh.devices.reshape(SIZES), AXES)
    in_specs = (P(AXES, None), P(FSDP, None, None), P(FSDP), P(FSDP), P(AXES, None))
    out_specs = (P(AXES, None), P(AXES, None), P(FSDP, None, None))
    return jax.shard_map(
        per_device, mesh=cut, in_specs=in_specs, out_specs=out_specs, check_vma=False
    )
```

```python
import functools

import jax
import jax.numpy as jnp
from jax import lax
from jax.experimental import pallas as pl
from jax.experimental.pallas import tpu as pltpu
from jax.sharding import Mesh, PartitionSpec as P

AXES = ("yh", "z", "c", "x", "yl")
SIZES = (2, 16, 2, 4, 2)
FSDP = ("yh", "z", "c")
REP = ("x", "yl")
PLANE = ("yh", "x", "yl")
B = 128
NNZ, RB, CB = 64, 32, 8


def vmem_mib(limit):
    return pltpu.CompilerParams(vmem_limit_bytes=limit * 1024 * 1024)


def grads_kernel(parity_ref, code_ref, x_ref, g_ref, out_ref):
    parity = parity_ref[0]
    for yh in range(2):
        for z in range(16):
            code = code_ref[yh * 32 + z * 2 + parity]
            row = pl.multiple_of((code // CB) * B, B)
            col = pl.multiple_of((code % CB) * B, B)
            grad = lax.dot_general(
                x_ref[:, pl.ds(row, B)],
                g_ref[:, pl.ds(col, B)],
                (((0,), (0,)), ((), ())),
                preferred_element_type=jnp.float32,
            )
            out_ref[yh * 8 : (yh + 1) * 8, z] = grad.reshape(8, 16, B)


def packet_kernel(rep_ref, row_ref, column_ref, blocks_ref, out_ref, wide):
    wide[...] = blocks_ref[0].astype(jnp.float32)
    code = jnp.full((2, B), row_ref[0] * CB + column_ref[0], jnp.int32).astype(jnp.float32)
    for yh in range(2):
        for odd in range(2):
            for core in range(2):
                at = core * 32 + odd * 16 + yh * 8 + rep_ref[0]
                rows = [wide[pl.ds(at, 1), :], wide[pl.ds(64 + at, 1), :], code]
                piece = jnp.concatenate(rows, axis=0).astype(jnp.bfloat16)
                for z in range(odd, 16, 2):
                    out_ref[yh * 32 + z * 2 + core] = piece


def make_packet(rep, row, column, blocks):
    smem = pl.BlockSpec(memory_space=pltpu.SMEM)
    vmem = pl.BlockSpec(memory_space=pltpu.VMEM)
    return pl.pallas_call(
        packet_kernel,
        out_shape=jax.ShapeDtypeStruct((NNZ, 4, B), jnp.bfloat16),
        in_specs=[smem, smem, smem, vmem],
        out_specs=vmem,
        scratch_shapes=[pltpu.VMEM((B, B), jnp.float32)],
        compiler_params=vmem_mib(4),
        name="packet",
    )(rep, row, column, blocks)


def power_kernel(x_ref, g_ref, out_ref):
    tops = []
    for ref in (x_ref, g_ref):
        top = jnp.abs(ref[:16, :])
        for row in range(16, ref.shape[0], 16):
            top = jnp.maximum(top, jnp.abs(ref[row : row + 16, :]))
        tops.append(jnp.max(top.astype(jnp.float32), axis=(0, 1), keepdims=True))
    bound = x_ref.shape[0] * jnp.maximum(tops[0] * tops[1], 1e-30)
    power = jnp.floor(jnp.log2(16384.0 / bound))
    out_ref[...] = jnp.broadcast_to(power, out_ref.shape)


def own_power(x, g):
    vmem = pl.BlockSpec(memory_space=pltpu.VMEM)
    return pl.pallas_call(
        power_kernel,
        out_shape=jax.ShapeDtypeStruct((16, B), jnp.float32),
        in_specs=[vmem, vmem],
        out_specs=vmem,
        compiler_params=vmem_mib(8),
        name="power",
    )(x, g)


def half_grads(parity, codes, x, g):
    smem = pl.BlockSpec(memory_space=pltpu.SMEM)
    vmem = pl.BlockSpec(memory_space=pltpu.VMEM)
    return pl.pallas_call(
        grads_kernel,
        out_shape=jax.ShapeDtypeStruct((16, 16, 16, B), jnp.float32),
        in_specs=[smem, smem, vmem, vmem],
        out_specs=vmem,
        compiler_params=vmem_mib(8),
        name="block_grads",
    )(parity.reshape(1), codes, x, g)


def share_kernel(got_ref, power_ref, share_ref, wide):
    wide[...] = got_ref[...].astype(jnp.float32).reshape(NNZ * 4, B)
    power = jnp.concatenate([power_ref[...]] * 2, axis=0).astype(jnp.bfloat16)
    for i in range(2):
        rows = wide[pl.ds(i, NNZ, stride=4), :].astype(jnp.bfloat16)
        for copy in range(16):
            share_ref[copy, i * NNZ : (i + 1) * NNZ, :] = rows
    for copy in range(16):
        share_ref[copy, 2 * NNZ :, :] = power


def share_copies(got, power):
    vmem = pl.BlockSpec(memory_space=pltpu.VMEM)
    return pl.pallas_call(
        share_kernel,
        out_shape=jax.ShapeDtypeStruct((16, 2 * NNZ + 16, B), jnp.bfloat16),
        in_specs=[vmem, vmem],
        out_specs=vmem,
        scratch_shapes=[pltpu.VMEM((NNZ * 4, B), jnp.float32)],
        compiler_params=vmem_mib(4),
        name="share",
    )(got, power)


def stage_kernel(parity_ref, near_ref, up_ref, down_ref, w_ref, wide):
    for s in range(16):
        beside = (up_ref if s < 8 else down_ref).at[s % 8]
        for slot, at in ((near_ref.at[s], parity_ref[0]), (beside, 1 - parity_ref[0])):
            wide[pl.ds(pl.multiple_of((at * 16 + s) * B, B), B), :] = slot[:B].astype(
                jnp.float32
            )
    for n in range(NNZ):
        for i in range(2):
            w_ref[n, i * 32 : (i + 1) * 32, :] = wide[
                pl.ds(i * NNZ + n, 32, stride=B), :
            ].astype(jnp.bfloat16)


def stage(parity, near, up, down):
    vmem = pl.BlockSpec(memory_space=pltpu.VMEM)
    smem = pl.BlockSpec(memory_space=pltpu.SMEM)
    return pl.pallas_call(
        stage_kernel,
        out_shape=jax.ShapeDtypeStruct((NNZ, B // 2, B), jnp.bfloat16),
        in_specs=[smem, vmem, vmem, vmem],
        out_specs=vmem,
        scratch_shapes=[pltpu.VMEM((32 * B, B), jnp.float32)],
        compiler_params=vmem_mib(8),
        name="stage",
    )(parity, near, up, down)


def order_kernel(code_ref, by_col, by_row, fill):
    for k in range(CB + RB):
        fill[k] = 0
    for n in range(NNZ):
        code = code_ref[n]
        row, col = code // CB, code % CB
        at = fill[col]
        by_col[col * 8 + at] = n
        fill[col] = at + 1
        at = fill[CB + row]
        by_row[row * 2 + at] = n
        fill[CB + row] = at + 1


def order_blocks(codes):
    smem = pl.BlockSpec(memory_space=pltpu.SMEM)
    order = jax.ShapeDtypeStruct((NNZ,), jnp.int32)
    return pl.pallas_call(
        order_kernel,
        out_shape=[order, order],
        in_specs=[smem],
        out_specs=[smem, smem],
        scratch_shapes=[pltpu.SMEM((CB + RB,), jnp.int32)],
        name="order",
    )(codes)


def project_kernel(core_ref, code_ref, by_col, by_row, x_ref, g_ref, near_ref, far_ref, v_out, d_out, w, v, d, sems):
    for half_ref, core in ((near_ref, core_ref[0]), (far_ref, 1 - core_ref[0])):
        for i in range(2):
            at = pl.multiple_of(i * 64 + core * 32, 32)
            w[:, pl.ds(at, 32), :] = half_ref[:, i * 32 : (i + 1) * 32, :]

    copies = []
    for row in range(RB):
        ns = [by_row[row * 2 + k] for k in range(2)]
        cols = [code_ref[n] % CB for n in ns]
        gs = jnp.concatenate(
            [g_ref[:, pl.ds(pl.multiple_of(c * B, B), B)] for c in cols], axis=1
        )
        ws = jnp.concatenate([w[n] for n in ns], axis=1)
        d[:, row * B : (row + 1) * B] = lax.dot_general(
            gs, ws, (((1,), (1,)), ((), ())), preferred_element_type=jnp.float32
        ).astype(d.dtype)
        if row % 8 == 7:
            span = pl.ds((row - 7) * B, 8 * B)
            copies.append(
                pltpu.make_async_copy(d.at[:, span], d_out.at[:, span], sems.at[row // 8])
            )
            copies[-1].start()
    for col in range(CB):
        ns = [by_col[col * 8 + k] for k in range(8)]
        rows = [code_ref[n] // CB for n in ns]
        xs = jnp.concatenate(
            [x_ref[:, pl.ds(pl.multiple_of(r * B, B), B)] for r in rows], axis=1
        )
        ws = jnp.concatenate([w[n] for n in ns], axis=0)
        v[:, col * B : (col + 1) * B] = jnp.dot(
            xs, ws, preferred_element_type=jnp.float32
        ).astype(v.dtype)
        if col % 4 == 3:
            span = pl.ds((col - 3) * B, 4 * B)
            copies.append(
                pltpu.make_async_copy(v.at[:, span], v_out.at[:, span], sems.at[4 + col // 4])
            )
            copies[-1].start()
    for copy in copies:
        copy.wait()


def project(core, codes, by_col, by_row, x, g, near, far):
    smem = pl.BlockSpec(memory_space=pltpu.SMEM)
    vmem = pl.BlockSpec(memory_space=pltpu.VMEM)
    hbm = pl.BlockSpec(memory_space=pl.ANY)
    return pl.pallas_call(
        project_kernel,
        out_shape=[
            jax.ShapeDtypeStruct(g.shape, jnp.bfloat16),
            jax.ShapeDtypeStruct(x.shape, jnp.bfloat16),
        ],
        in_specs=[smem] * 4 + [vmem] * 4,
        out_specs=[hbm, hbm],
        scratch_shapes=[
            pltpu.VMEM((NNZ, B, B), jnp.bfloat16),
            pltpu.VMEM(g.shape, jnp.bfloat16),
            pltpu.VMEM(x.shape, jnp.bfloat16),
            pltpu.SemaphoreType.DMA((6,)),
        ],
        compiler_params=vmem_mib(20),
        name="project",
    )(core, codes, by_col, by_row, x, g, near, far)


def flip(value, axis, by=1):
    size = lax.axis_size(axis)
    return lax.ppermute(value, axis, [(i, i ^ by) for i in range(size)])


def to_all(part, axes, count):
    return lax.all_to_all(
        jnp.broadcast_to(part[None], (count,) + part.shape), axes, 0, 0, tiled=True
    )


def per_device(x, blocks, block_row, block_column, g):
    core = lax.axis_index("c").astype(jnp.int32)
    rep = lax.axis_index(REP).astype(jnp.int32).reshape(1)
    packet = make_packet(rep, block_row, block_column, blocks)
    got = lax.all_to_all(packet, FSDP, 0, 0, tiled=True)

    power = own_power(x, g)
    power = jnp.minimum(power, flip(power, "c"))
    got, power = lax.optimization_barrier((got, power))

    share = share_copies(got, power[:8])
    near = lax.all_to_all(share, PLANE, 0, 0, tiled=True)

    def grads(got, power, x, g):
        codes = got[:, 2, 0].astype(jnp.int32)
        up = jnp.exp2(power)
        outgoing = (half_grads(1 - core, codes, x, g) * up).astype(jnp.float16)
        incoming = flip(outgoing, "c").astype(jnp.float32)
        own = half_grads(core, codes, x, g)
        return (own * up + incoming).astype(jnp.float16), codes

    def nothing(got, power, x, g):
        return jnp.zeros((16, 16, 16, B), jnp.float16), jnp.zeros((NNZ,), jnp.int32)

    paired, codes = lax.cond(block_row[0] < RB, grads, nothing, got, power, x, g)
    paired, near = lax.optimization_barrier((paired, near))
    spread = lax.all_to_all(paired, PLANE, 0, 0, tiled=True)
    parity = (lax.axis_index("z") % 2).astype(jnp.int32).reshape(1)
    from_below = lax.ppermute(near[:8], "z", [(i, (i + 1) % 16) for i in range(16)])
    from_above = lax.ppermute(near[8:], "z", [(i, (i - 1) % 16) for i in range(16)])
    by_col, by_row = order_blocks(codes)
    spread, from_below, from_above, by_col, by_row = lax.optimization_barrier(
        (spread, from_below, from_above, by_col, by_row)
    )
    down = jnp.exp2(-near[:, B:].astype(jnp.float32))
    plane_sum = jnp.sum(spread.astype(jnp.float32) * down[:, None], axis=0)

    def halves(near, from_below, from_above):
        half = stage(parity, near, from_below, from_above)
        return half, flip(half, "c")

    def no_halves(near, from_below, from_above):
        half = jnp.zeros((NNZ, B // 2, B), jnp.bfloat16)
        return half, half

    ring = lax.all_to_all(plane_sum, "z", 0, 0, tiled=True)
    half, far = lax.cond(block_row[0] < RB, halves, no_halves, near, from_below, from_above)
    ring, half, far = lax.optimization_barrier((ring, half, far))
    loss_scale = (x.shape[0] * lax.axis_size(AXES)) ** (-0.5)
    strip = jnp.sum(ring, axis=0) * loss_scale
    weight_grad = to_all(strip, REP, 8).reshape(1, B, B)
    values_out, input_grad = project(core.reshape(1), codes, by_col, by_row, x, g, half, far)
    return values_out, input_grad, weight_grad


def solution(mesh):
    cut = Mesh(mesh.devices.reshape(SIZES), AXES)
    in_specs = (P(AXES, None), P(FSDP, None, None), P(FSDP), P(FSDP), P(AXES, None))
    out_specs = (P(AXES, None), P(AXES, None), P(FSDP, None, None))
    return jax.shard_map(
        per_device, mesh=cut, in_specs=in_specs, out_specs=out_specs, check_vma=False
    )
```

```python
import functools

import jax
import jax.numpy as jnp
from jax import lax
from jax.experimental import pallas as pl
from jax.experimental.pallas import tpu as pltpu
from jax.sharding import Mesh, PartitionSpec as P

AXES = ("yh", "z", "c", "x", "yl")
SIZES = (2, 16, 2, 4, 2)
FSDP = ("yh", "z", "c")
REP = ("x", "yl")
PLANE = ("yh", "x", "yl")
B = 128
NNZ, RB, CB = 64, 32, 8


def vmem_mib(limit):
    return pltpu.CompilerParams(vmem_limit_bytes=limit * 1024 * 1024)


def grads_kernel(parity_ref, code_ref, x_ref, g_ref, out_ref):
    parity = parity_ref[0]
    for yh in range(2):
        for z in range(16):
            code = code_ref[yh * 32 + z * 2 + parity]
            row = pl.multiple_of((code // CB) * B, B)
            col = pl.multiple_of((code % CB) * B, B)
            grad = lax.dot_general(
                x_ref[:, pl.ds(row, B)],
                g_ref[:, pl.ds(col, B)],
                (((0,), (0,)), ((), ())),
                preferred_element_type=jnp.float32,
            )
            out_ref[yh * 8 : (yh + 1) * 8, z] = grad.reshape(8, 16, B)


def packet_kernel(rep_ref, row_ref, column_ref, blocks_ref, out_ref, wide):
    wide[...] = blocks_ref[0].astype(jnp.float32)
    code = jnp.full((2, B), row_ref[0] * CB + column_ref[0], jnp.int32).astype(jnp.float32)
    for yh in range(2):
        for odd in range(2):
            for core in range(2):
                at = core * 32 + odd * 16 + yh * 8 + rep_ref[0]
                rows = [wide[pl.ds(at, 1), :], wide[pl.ds(64 + at, 1), :], code]
                piece = jnp.concatenate(rows, axis=0).astype(jnp.bfloat16)
                for z in range(odd, 16, 2):
                    out_ref[yh * 32 + z * 2 + core] = piece


def make_packet(rep, row, column, blocks):
    smem = pl.BlockSpec(memory_space=pltpu.SMEM)
    vmem = pl.BlockSpec(memory_space=pltpu.VMEM)
    return pl.pallas_call(
        packet_kernel,
        out_shape=jax.ShapeDtypeStruct((NNZ, 4, B), jnp.bfloat16),
        in_specs=[smem, smem, smem, vmem],
        out_specs=vmem,
        scratch_shapes=[pltpu.VMEM((B, B), jnp.float32)],
        compiler_params=vmem_mib(4),
        name="packet",
    )(rep, row, column, blocks)


def power_kernel(x_ref, g_ref, out_ref):
    tops = []
    for ref in (x_ref, g_ref):
        top = jnp.abs(ref[:16, :])
        for row in range(16, ref.shape[0], 16):
            top = jnp.maximum(top, jnp.abs(ref[row : row + 16, :]))
        tops.append(jnp.max(top.astype(jnp.float32), axis=(0, 1), keepdims=True))
    bound = x_ref.shape[0] * jnp.maximum(tops[0] * tops[1], 1e-30)
    power = jnp.floor(jnp.log2(16384.0 / bound))
    out_ref[...] = jnp.broadcast_to(power, out_ref.shape)


def own_power(x, g):
    vmem = pl.BlockSpec(memory_space=pltpu.VMEM)
    return pl.pallas_call(
        power_kernel,
        out_shape=jax.ShapeDtypeStruct((16, B), jnp.float32),
        in_specs=[vmem, vmem],
        out_specs=vmem,
        compiler_params=vmem_mib(8),
        name="power",
    )(x, g)


def half_grads(parity, codes, x, g):
    smem = pl.BlockSpec(memory_space=pltpu.SMEM)
    vmem = pl.BlockSpec(memory_space=pltpu.VMEM)
    return pl.pallas_call(
        grads_kernel,
        out_shape=jax.ShapeDtypeStruct((16, 16, 16, B), jnp.float32),
        in_specs=[smem, smem, vmem, vmem],
        out_specs=vmem,
        compiler_params=vmem_mib(8),
        name="block_grads",
    )(parity.reshape(1), codes, x, g)


def share_kernel(got_ref, power_ref, share_ref, wide):
    wide[...] = got_ref[...].astype(jnp.float32).reshape(NNZ * 4, B)
    power = jnp.concatenate([power_ref[...]] * 2, axis=0).astype(jnp.bfloat16)
    for i in range(2):
        rows = wide[pl.ds(i, NNZ, stride=4), :].astype(jnp.bfloat16)
        for copy in range(16):
            share_ref[copy, i * NNZ : (i + 1) * NNZ, :] = rows
    for copy in range(16):
        share_ref[copy, 2 * NNZ :, :] = power


def share_copies(got, power):
    vmem = pl.BlockSpec(memory_space=pltpu.VMEM)
    return pl.pallas_call(
        share_kernel,
        out_shape=jax.ShapeDtypeStruct((16, 2 * NNZ + 16, B), jnp.bfloat16),
        in_specs=[vmem, vmem],
        out_specs=vmem,
        scratch_shapes=[pltpu.VMEM((NNZ * 4, B), jnp.float32)],
        compiler_params=vmem_mib(4),
        name="share",
    )(got, power)


def stage_kernel(parity_ref, near_hbm, up_hbm, down_hbm, w_hbm, near, beside, wide, w, sems):
    loads = [
        pltpu.make_async_copy(near_hbm.at[:, :B], near, sems.at[0]),
        pltpu.make_async_copy(up_hbm.at[:, :B], beside.at[:8], sems.at[1]),
        pltpu.make_async_copy(down_hbm.at[:, :B], beside.at[8:], sems.at[2]),
    ]
    for load in loads:
        load.start()
    loads[0].wait()
    for slots, at in ((near, parity_ref[0]), (beside, 1 - parity_ref[0])):
        for s in range(16):
            if slots is beside and s % 8 == 0:
                loads[1 + s // 8].wait()
            wide[pl.ds(pl.multiple_of((at * 16 + s) * B, B), B), :] = slots[s].astype(
                jnp.float32
            )
    stores = []
    for n in range(NNZ):
        for i in range(2):
            w[n, i * 32 : (i + 1) * 32, :] = wide[
                pl.ds(i * NNZ + n, 32, stride=B), :
            ].astype(jnp.bfloat16)
        if n % 16 == 15:
            span = pl.ds(n - 15, 16)
            stores.append(pltpu.make_async_copy(w.at[span], w_hbm.at[span], sems.at[3 + n // 16]))
            stores[-1].start()
    for store in stores:
        store.wait()


def stage(parity, near, up, down):
    hbm = pl.BlockSpec(memory_space=pl.ANY)
    return pl.pallas_call(
        stage_kernel,
        out_shape=jax.ShapeDtypeStruct((NNZ, B // 2, B), jnp.bfloat16),
        in_specs=[pl.BlockSpec(memory_space=pltpu.SMEM), hbm, hbm, hbm],
        out_specs=hbm,
        scratch_shapes=[
            pltpu.VMEM((16, B, B), jnp.bfloat16),
            pltpu.VMEM((16, B, B), jnp.bfloat16),
            pltpu.VMEM((32 * B, B), jnp.float32),
            pltpu.VMEM((NNZ, B // 2, B), jnp.bfloat16),
            pltpu.SemaphoreType.DMA((7,)),
        ],
        compiler_params=vmem_mib(10),
        name="stage",
    )(parity, near, up, down)


def order_kernel(code_ref, near_hbm, by_col, by_row, down_ref, lift_ref, fill, powers, sem):
    load = pltpu.make_async_copy(near_hbm.at[:, B:], powers, sem)
    load.start()
    for k in range(CB + RB):
        fill[k] = 0
    for n in range(NNZ):
        code = code_ref[n]
        row, col = code // CB, code % CB
        at = fill[col]
        by_col[col * 8 + at] = n
        fill[col] = at + 1
        at = fill[CB + row]
        by_row[row * 2 + at] = n
        fill[CB + row] = at + 1
    load.wait()
    lift = jnp.min(powers[...].astype(jnp.float32), axis=0) - 4.0
    down_ref[...] = jnp.exp2(lift[None] - powers[...].astype(jnp.float32))
    lift_ref[...] = lift


def order_blocks(codes, near):
    smem = pl.BlockSpec(memory_space=pltpu.SMEM)
    order = jax.ShapeDtypeStruct((NNZ,), jnp.int32)
    return pl.pallas_call(
        order_kernel,
        out_shape=[
            order,
            order,
            jax.ShapeDtypeStruct((16, 16, B), jnp.float32),
            jax.ShapeDtypeStruct((16, B), jnp.float32),
        ],
        in_specs=[smem, pl.BlockSpec(memory_space=pl.ANY)],
        out_specs=[smem, smem] + [pl.BlockSpec(memory_space=pltpu.VMEM)] * 2,
        scratch_shapes=[
            pltpu.SMEM((CB + RB,), jnp.int32),
            pltpu.VMEM((16, 16, B), jnp.bfloat16),
            pltpu.SemaphoreType.DMA,
        ],
        compiler_params=vmem_mib(4),
        name="order",
    )(codes, near)


def project_kernel(core_ref, code_ref, by_col, by_row, x_ref, g_ref, near_ref, far_ref, v_out, d_out, w, v, d, sems):
    for half_ref, core in ((near_ref, core_ref[0]), (far_ref, 1 - core_ref[0])):
        for i in range(2):
            at = pl.multiple_of(i * 64 + core * 32, 32)
            w[:, pl.ds(at, 32), :] = half_ref[:, i * 32 : (i + 1) * 32, :]

    copies = []
    for row in range(RB):
        ns = [by_row[row * 2 + k] for k in range(2)]
        cols = [code_ref[n] % CB for n in ns]
        gs = jnp.concatenate(
            [g_ref[:, pl.ds(pl.multiple_of(c * B, B), B)] for c in cols], axis=1
        )
        ws = jnp.concatenate([w[n] for n in ns], axis=1)
        d[:, row * B : (row + 1) * B] = lax.dot_general(
            gs, ws, (((1,), (1,)), ((), ())), preferred_element_type=jnp.float32
        ).astype(d.dtype)
        if row % 8 == 7:
            span = pl.ds((row - 7) * B, 8 * B)
            copies.append(
                pltpu.make_async_copy(d.at[:, span], d_out.at[:, span], sems.at[row // 8])
            )
            copies[-1].start()
    for col in range(CB):
        ns = [by_col[col * 8 + k] for k in range(8)]
        rows = [code_ref[n] // CB for n in ns]
        xs = jnp.concatenate(
            [x_ref[:, pl.ds(pl.multiple_of(r * B, B), B)] for r in rows], axis=1
        )
        ws = jnp.concatenate([w[n] for n in ns], axis=0)
        v[:, col * B : (col + 1) * B] = jnp.dot(
            xs, ws, preferred_element_type=jnp.float32
        ).astype(v.dtype)
        if col % 4 == 3:
            span = pl.ds((col - 3) * B, 4 * B)
            copies.append(
                pltpu.make_async_copy(v.at[:, span], v_out.at[:, span], sems.at[4 + col // 4])
            )
            copies[-1].start()
    for copy in copies:
        copy.wait()


def project(core, codes, by_col, by_row, x, g, near, far):
    smem = pl.BlockSpec(memory_space=pltpu.SMEM)
    vmem = pl.BlockSpec(memory_space=pltpu.VMEM)
    hbm = pl.BlockSpec(memory_space=pl.ANY)
    return pl.pallas_call(
        project_kernel,
        out_shape=[
            jax.ShapeDtypeStruct(g.shape, jnp.bfloat16),
            jax.ShapeDtypeStruct(x.shape, jnp.bfloat16),
        ],
        in_specs=[smem] * 4 + [vmem] * 4,
        out_specs=[hbm, hbm],
        scratch_shapes=[
            pltpu.VMEM((NNZ, B, B), jnp.bfloat16),
            pltpu.VMEM(g.shape, jnp.bfloat16),
            pltpu.VMEM(x.shape, jnp.bfloat16),
            pltpu.SemaphoreType.DMA((6,)),
        ],
        compiler_params=vmem_mib(20),
        name="project",
    )(core, codes, by_col, by_row, x, g, near, far)


def flip(value, axis, by=1):
    size = lax.axis_size(axis)
    return lax.ppermute(value, axis, [(i, i ^ by) for i in range(size)])


def to_all(part, axes, count):
    return lax.all_to_all(
        jnp.broadcast_to(part[None], (count,) + part.shape), axes, 0, 0, tiled=True
    )


def per_device(x, blocks, block_row, block_column, g):
    core = lax.axis_index("c").astype(jnp.int32)
    rep = lax.axis_index(REP).astype(jnp.int32).reshape(1)
    packet = make_packet(rep, block_row, block_column, blocks)
    got = lax.all_to_all(packet, FSDP, 0, 0, tiled=True)

    power = own_power(x, g)
    power = jnp.minimum(power, flip(power, "c"))
    got, power = lax.optimization_barrier((got, power))

    share = share_copies(got, power[:8])
    near = lax.all_to_all(share, PLANE, 0, 0, tiled=True)

    def grads(got, power, x, g):
        codes = got[:, 2, 0].astype(jnp.int32)
        up = jnp.exp2(power)
        outgoing = (half_grads(1 - core, codes, x, g) * up).astype(jnp.float16)
        incoming = flip(outgoing, "c").astype(jnp.float32)
        own = half_grads(core, codes, x, g)
        return (own * up + incoming).astype(jnp.float16), codes

    def nothing(got, power, x, g):
        return jnp.zeros((16, 16, 16, B), jnp.float16), jnp.zeros((NNZ,), jnp.int32)

    paired, codes = lax.cond(block_row[0] < RB, grads, nothing, got, power, x, g)
    paired, near = lax.optimization_barrier((paired, near))
    spread = lax.all_to_all(paired, PLANE, 0, 0, tiled=True)
    parity = (lax.axis_index("z") % 2).astype(jnp.int32).reshape(1)
    from_below = lax.ppermute(near[:8], "z", [(i, (i + 1) % 16) for i in range(16)])
    from_above = lax.ppermute(near[8:], "z", [(i, (i - 1) % 16) for i in range(16)])
    by_col, by_row, down, lift = order_blocks(codes, near)
    spread, from_below, from_above, by_col, by_row, down, lift = lax.optimization_barrier(
        (spread, from_below, from_above, by_col, by_row, down, lift)
    )
    plane_sum = jnp.sum(spread.astype(jnp.float32) * down[:, None], axis=0)
    tail = jnp.broadcast_to(lift[None, :8], (16, 8, B))
    plane_sum = jnp.concatenate([plane_sum, tail], axis=1).astype(jnp.float16)

    def halves(near, from_below, from_above):
        half = stage(parity, near, from_below, from_above)
        return half, flip(half, "c")

    def no_halves(near, from_below, from_above):
        half = jnp.zeros((NNZ, B // 2, B), jnp.bfloat16)
        return half, half

    ring = lax.all_to_all(plane_sum, "z", 0, 0, tiled=True)
    half, far = lax.cond(block_row[0] < RB, halves, no_halves, near, from_below, from_above)
    ring, half, far = lax.optimization_barrier((ring, half, far))
    loss_scale = (x.shape[0] * lax.axis_size(AXES)) ** (-0.5)
    ring = ring.astype(jnp.float32)
    strip = jnp.sum(ring[:, :16] * jnp.exp2(-ring[:, 16:17]), axis=0) * loss_scale
    weight_grad = to_all(strip, REP, 8).reshape(1, B, B)
    values_out, input_grad = project(core.reshape(1), codes, by_col, by_row, x, g, half, far)
    return values_out, input_grad, weight_grad


def solution(mesh):
    cut = Mesh(mesh.devices.reshape(SIZES), AXES)
    in_specs = (P(AXES, None), P(FSDP, None, None), P(FSDP), P(FSDP), P(AXES, None))
    out_specs = (P(AXES, None), P(AXES, None), P(FSDP, None, None))
    return jax.shard_map(
        per_device, mesh=cut, in_specs=in_specs, out_specs=out_specs, check_vma=False
    )
```

```python
import functools

import jax
import jax.numpy as jnp
from jax import lax
from jax.experimental import pallas as pl
from jax.experimental.pallas import tpu as pltpu
from jax.sharding import Mesh, PartitionSpec as P

AXES = ("yh", "z", "c", "x", "yl")
SIZES = (2, 16, 2, 4, 2)
FSDP = ("yh", "z", "c")
REP = ("x", "yl")
PLANE = ("yh", "x", "yl")
B = 128
NNZ, RB, CB = 64, 32, 8


def vmem_mib(limit):
    return pltpu.CompilerParams(vmem_limit_bytes=limit * 1024 * 1024)


def grads_kernel(parity_ref, code_ref, x_ref, g_ref, out_ref):
    parity = parity_ref[0]
    for yh in range(2):
        for z in range(16):
            code = code_ref[yh * 32 + z * 2 + parity]
            row = pl.multiple_of((code // CB) * B, B)
            col = pl.multiple_of((code % CB) * B, B)
            grad = lax.dot_general(
                x_ref[:, pl.ds(row, B)],
                g_ref[:, pl.ds(col, B)],
                (((0,), (0,)), ((), ())),
                preferred_element_type=jnp.float32,
            )
            out_ref[yh * 8 : (yh + 1) * 8, z] = grad.reshape(8, 16, B)


def packet_kernel(rep_ref, row_ref, column_ref, blocks_ref, out_ref, wide):
    wide[...] = blocks_ref[0].astype(jnp.float32)
    code = jnp.full((2, B), row_ref[0] * CB + column_ref[0], jnp.int32).astype(jnp.float32)
    for yh in range(2):
        for odd in range(2):
            for core in range(2):
                at = core * 32 + odd * 16 + yh * 8 + rep_ref[0]
                rows = [wide[pl.ds(at, 1), :], wide[pl.ds(64 + at, 1), :], code]
                piece = jnp.concatenate(rows, axis=0).astype(jnp.bfloat16)
                for z in range(odd, 16, 2):
                    out_ref[yh * 32 + z * 2 + core] = piece


def make_packet(rep, row, column, blocks):
    smem = pl.BlockSpec(memory_space=pltpu.SMEM)
    vmem = pl.BlockSpec(memory_space=pltpu.VMEM)
    return pl.pallas_call(
        packet_kernel,
        out_shape=jax.ShapeDtypeStruct((NNZ, 4, B), jnp.bfloat16),
        in_specs=[smem, smem, smem, vmem],
        out_specs=vmem,
        scratch_shapes=[pltpu.VMEM((B, B), jnp.float32)],
        compiler_params=vmem_mib(4),
        name="packet",
    )(rep, row, column, blocks)


def power_kernel(x_ref, g_ref, out_ref):
    tops = []
    for ref in (x_ref, g_ref):
        top = jnp.abs(ref[:16, :])
        for row in range(16, ref.shape[0], 16):
            top = jnp.maximum(top, jnp.abs(ref[row : row + 16, :]))
        tops.append(jnp.max(top.astype(jnp.float32), axis=(0, 1), keepdims=True))
    bound = x_ref.shape[0] * jnp.maximum(tops[0] * tops[1], 1e-30)
    power = jnp.floor(jnp.log2(16384.0 / bound))
    out_ref[...] = jnp.broadcast_to(power, out_ref.shape)


def own_power(x, g):
    vmem = pl.BlockSpec(memory_space=pltpu.VMEM)
    return pl.pallas_call(
        power_kernel,
        out_shape=jax.ShapeDtypeStruct((16, B), jnp.float32),
        in_specs=[vmem, vmem],
        out_specs=vmem,
        compiler_params=vmem_mib(8),
        name="power",
    )(x, g)


def half_grads(parity, codes, x, g):
    smem = pl.BlockSpec(memory_space=pltpu.SMEM)
    vmem = pl.BlockSpec(memory_space=pltpu.VMEM)
    return pl.pallas_call(
        grads_kernel,
        out_shape=jax.ShapeDtypeStruct((16, 16, 16, B), jnp.float32),
        in_specs=[smem, smem, vmem, vmem],
        out_specs=vmem,
        compiler_params=vmem_mib(8),
        name="block_grads",
    )(parity.reshape(1), codes, x, g)


def share_kernel(got_ref, power_ref, share_ref, wide):
    wide[...] = got_ref[...].astype(jnp.float32).reshape(NNZ * 4, B)
    power = jnp.concatenate([power_ref[...]] * 2, axis=0).astype(jnp.bfloat16)
    for i in range(2):
        rows = wide[pl.ds(i, NNZ, stride=4), :].astype(jnp.bfloat16)
        for copy in range(16):
            share_ref[copy, i * NNZ : (i + 1) * NNZ, :] = rows
    for copy in range(16):
        share_ref[copy, 2 * NNZ :, :] = power


def share_copies(got, power):
    vmem = pl.BlockSpec(memory_space=pltpu.VMEM)
    return pl.pallas_call(
        share_kernel,
        out_shape=jax.ShapeDtypeStruct((16, 2 * NNZ + 16, B), jnp.bfloat16),
        in_specs=[vmem, vmem],
        out_specs=vmem,
        scratch_shapes=[pltpu.VMEM((NNZ * 4, B), jnp.float32)],
        compiler_params=vmem_mib(4),
        name="share",
    )(got, power)


def stage_kernel(parity_ref, near_hbm, up_hbm, down_hbm, w_hbm, near, beside, wide, w, sems):
    loads = [
        pltpu.make_async_copy(near_hbm.at[:, :B], near, sems.at[0]),
        pltpu.make_async_copy(up_hbm.at[:, :B], beside.at[:8], sems.at[1]),
        pltpu.make_async_copy(down_hbm.at[:, :B], beside.at[8:], sems.at[2]),
    ]
    for load in loads:
        load.start()
    loads[0].wait()
    for slots, at in ((near, parity_ref[0]), (beside, 1 - parity_ref[0])):
        for s in range(16):
            if slots is beside and s % 8 == 0:
                loads[1 + s // 8].wait()
            wide[pl.ds(pl.multiple_of((at * 16 + s) * B, B), B), :] = slots[s].astype(
                jnp.float32
            )
    stores = []
    for n in range(NNZ):
        for i in range(2):
            w[n, i * 32 : (i + 1) * 32, :] = wide[
                pl.ds(i * NNZ + n, 32, stride=B), :
            ].astype(jnp.bfloat16)
        if n % 16 == 15:
            span = pl.ds(n - 15, 16)
            stores.append(pltpu.make_async_copy(w.at[span], w_hbm.at[span], sems.at[3 + n // 16]))
            stores[-1].start()
    for store in stores:
        store.wait()


def stage(parity, near, up, down):
    hbm = pl.BlockSpec(memory_space=pl.ANY)
    return pl.pallas_call(
        stage_kernel,
        out_shape=jax.ShapeDtypeStruct((NNZ, B // 2, B), jnp.bfloat16),
        in_specs=[pl.BlockSpec(memory_space=pltpu.SMEM), hbm, hbm, hbm],
        out_specs=hbm,
        scratch_shapes=[
            pltpu.VMEM((16, B, B), jnp.bfloat16),
            pltpu.VMEM((16, B, B), jnp.bfloat16),
            pltpu.VMEM((32 * B, B), jnp.float32),
            pltpu.VMEM((NNZ, B // 2, B), jnp.bfloat16),
            pltpu.SemaphoreType.DMA((7,)),
        ],
        compiler_params=vmem_mib(10),
        name="stage",
    )(parity, near, up, down)


def order_kernel(code_ref, near_hbm, by_col, by_row, down_ref, fill, powers, sem):
    load = pltpu.make_async_copy(near_hbm.at[:, B:], powers, sem)
    load.start()
    for k in range(CB + RB):
        fill[k] = 0
    for n in range(NNZ):
        code = code_ref[n]
        row, col = code // CB, code % CB
        at = fill[col]
        by_col[col * 8 + at] = n
        fill[col] = at + 1
        at = fill[CB + row]
        by_row[row * 2 + at] = n
        fill[CB + row] = at + 1
    load.wait()
    lift = jnp.min(powers[...].astype(jnp.float32), axis=0) - 4.0
    down_ref[:, :16] = jnp.exp2(lift[None] - powers[...].astype(jnp.float32))
    down_ref[:, 16:] = jnp.broadcast_to(lift[None, :8] / 16.0, (16, 8, B))


def order_blocks(codes, near):
    smem = pl.BlockSpec(memory_space=pltpu.SMEM)
    order = jax.ShapeDtypeStruct((NNZ,), jnp.int32)
    return pl.pallas_call(
        order_kernel,
        out_shape=[
            order,
            order,
            jax.ShapeDtypeStruct((16, 24, B), jnp.float32),
        ],
        in_specs=[smem, pl.BlockSpec(memory_space=pl.ANY)],
        out_specs=[smem, smem, pl.BlockSpec(memory_space=pltpu.VMEM)],
        scratch_shapes=[
            pltpu.SMEM((CB + RB,), jnp.int32),
            pltpu.VMEM((16, 16, B), jnp.bfloat16),
            pltpu.SemaphoreType.DMA,
        ],
        compiler_params=vmem_mib(4),
        name="order",
    )(codes, near)


def project_kernel(core_ref, code_ref, by_col, by_row, x_ref, g_ref, near_ref, far_ref, v_out, d_out, w, v, d, sems):
    for half_ref, core in ((near_ref, core_ref[0]), (far_ref, 1 - core_ref[0])):
        for i in range(2):
            at = pl.multiple_of(i * 64 + core * 32, 32)
            w[:, pl.ds(at, 32), :] = half_ref[:, i * 32 : (i + 1) * 32, :]

    copies = []
    for row in range(RB):
        ns = [by_row[row * 2 + k] for k in range(2)]
        cols = [code_ref[n] % CB for n in ns]
        gs = jnp.concatenate(
            [g_ref[:, pl.ds(pl.multiple_of(c * B, B), B)] for c in cols], axis=1
        )
        ws = jnp.concatenate([w[n] for n in ns], axis=1)
        d[:, row * B : (row + 1) * B] = lax.dot_general(
            gs, ws, (((1,), (1,)), ((), ())), preferred_element_type=jnp.float32
        ).astype(d.dtype)
        if row % 8 == 7:
            span = pl.ds((row - 7) * B, 8 * B)
            copies.append(
                pltpu.make_async_copy(d.at[:, span], d_out.at[:, span], sems.at[row // 8])
            )
            copies[-1].start()
    for col in range(CB):
        ns = [by_col[col * 8 + k] for k in range(8)]
        rows = [code_ref[n] // CB for n in ns]
        xs = jnp.concatenate(
            [x_ref[:, pl.ds(pl.multiple_of(r * B, B), B)] for r in rows], axis=1
        )
        ws = jnp.concatenate([w[n] for n in ns], axis=0)
        v[:, col * B : (col + 1) * B] = jnp.dot(
            xs, ws, preferred_element_type=jnp.float32
        ).astype(v.dtype)
        if col % 4 == 3:
            span = pl.ds((col - 3) * B, 4 * B)
            copies.append(
                pltpu.make_async_copy(v.at[:, span], v_out.at[:, span], sems.at[4 + col // 4])
            )
            copies[-1].start()
    for copy in copies:
        copy.wait()


def project(core, codes, by_col, by_row, x, g, near, far):
    smem = pl.BlockSpec(memory_space=pltpu.SMEM)
    vmem = pl.BlockSpec(memory_space=pltpu.VMEM)
    hbm = pl.BlockSpec(memory_space=pl.ANY)
    return pl.pallas_call(
        project_kernel,
        out_shape=[
            jax.ShapeDtypeStruct(g.shape, jnp.bfloat16),
            jax.ShapeDtypeStruct(x.shape, jnp.bfloat16),
        ],
        in_specs=[smem] * 4 + [vmem] * 4,
        out_specs=[hbm, hbm],
        scratch_shapes=[
            pltpu.VMEM((NNZ, B, B), jnp.bfloat16),
            pltpu.VMEM(g.shape, jnp.bfloat16),
            pltpu.VMEM(x.shape, jnp.bfloat16),
            pltpu.SemaphoreType.DMA((6,)),
        ],
        compiler_params=vmem_mib(20),
        name="project",
    )(core, codes, by_col, by_row, x, g, near, far)


def flip(value, axis, by=1):
    size = lax.axis_size(axis)
    return lax.ppermute(value, axis, [(i, i ^ by) for i in range(size)])


def to_all(part, axes, count):
    return lax.all_to_all(
        jnp.broadcast_to(part[None], (count,) + part.shape), axes, 0, 0, tiled=True
    )


def per_device(x, blocks, block_row, block_column, g):
    core = lax.axis_index("c").astype(jnp.int32)
    rep = lax.axis_index(REP).astype(jnp.int32).reshape(1)
    packet = make_packet(rep, block_row, block_column, blocks)
    got = lax.all_to_all(packet, FSDP, 0, 0, tiled=True)

    power = own_power(x, g)
    power = jnp.minimum(power, flip(power, "c"))
    got, power = lax.optimization_barrier((got, power))

    share = share_copies(got, power[:8])
    near = lax.all_to_all(share, PLANE, 0, 0, tiled=True)

    def grads(got, power, x, g):
        codes = got[:, 2, 0].astype(jnp.int32)
        up = jnp.exp2(power)
        outgoing = (half_grads(1 - core, codes, x, g) * up).astype(jnp.float16)
        incoming = flip(outgoing, "c").astype(jnp.float32)
        own = half_grads(core, codes, x, g)
        return (own * up + incoming).astype(jnp.float16), codes

    def nothing(got, power, x, g):
        return jnp.zeros((16, 16, 16, B), jnp.float16), jnp.zeros((NNZ,), jnp.int32)

    paired, codes = lax.cond(block_row[0] < RB, grads, nothing, got, power, x, g)
    paired, near = lax.optimization_barrier((paired, near))
    spread = lax.all_to_all(paired, PLANE, 0, 0, tiled=True)
    parity = (lax.axis_index("z") % 2).astype(jnp.int32).reshape(1)
    from_below = lax.ppermute(near[:8], "z", [(i, (i + 1) % 16) for i in range(16)])
    from_above = lax.ppermute(near[8:], "z", [(i, (i - 1) % 16) for i in range(16)])
    by_col, by_row, down = order_blocks(codes, near)
    spread, from_below, from_above, by_col, by_row, down = lax.optimization_barrier(
        (spread, from_below, from_above, by_col, by_row, down)
    )
    padded = jnp.pad(spread, ((0, 0), (0, 0), (0, 8), (0, 0)), constant_values=1)
    plane_sum = jnp.sum(padded.astype(jnp.float32) * down[:, None], axis=0)
    plane_sum = plane_sum.astype(jnp.float16)

    def halves(near, from_below, from_above):
        half = stage(parity, near, from_below, from_above)
        return half, flip(half, "c")

    def no_halves(near, from_below, from_above):
        half = jnp.zeros((NNZ, B // 2, B), jnp.bfloat16)
        return half, half

    ring = lax.all_to_all(plane_sum, "z", 0, 0, tiled=True)
    half, far = lax.cond(block_row[0] < RB, halves, no_halves, near, from_below, from_above)
    ring, half, far = lax.optimization_barrier((ring, half, far))
    loss_scale = (x.shape[0] * lax.axis_size(AXES)) ** (-0.5)
    ring = ring.astype(jnp.float32)
    strip = jnp.sum(ring[:, :16] * jnp.exp2(-ring[:, 16:17]), axis=0) * loss_scale
    weight_grad = to_all(strip, REP, 8).reshape(1, B, B)
    values_out, input_grad = project(core.reshape(1), codes, by_col, by_row, x, g, half, far)
    return values_out, input_grad, weight_grad


def solution(mesh):
    cut = Mesh(mesh.devices.reshape(SIZES), AXES)
    in_specs = (P(AXES, None), P(FSDP, None, None), P(FSDP), P(FSDP), P(AXES, None))
    out_specs = (P(AXES, None), P(AXES, None), P(FSDP, None, None))
    return jax.shard_map(
        per_device, mesh=cut, in_specs=in_specs, out_specs=out_specs, check_vma=False
    )
```
